32 devices in a mesh: clip: 2 (over x), blk: 16 (over z, y, core).
Axes of the slice: x: 2, y: 2, z: 4, core: 2. Of those that a mesh axis runs over, the one named last changes fastest.
Arguments:
- queries: bfloat16 [8192, 2560], P(('clip', 'blk')), parts along dimension 0, may hold values from -24 to 24
- keys: bfloat16 [8192, 2560], P(('clip', 'blk')), parts along dimension 0, may hold values from -24 to 24
- values: bfloat16 [8192, 2560], P(('clip', 'blk')), parts along dimension 0, may hold values from -6 to 6
- kept_blocks: int32 [64, 8], P(('clip', 'blk')), parts along dimension 0, may hold values from 0 to 31, as said below
Outputs:
- attended: bfloat16 [8192, 2560], P(('clip', 'blk')), parts along dimension 0
The draws below stay inside these ranges and needn't reach their ends.
There are 2 independent parts, one for each index of `clip`. The reference program is written for one: setup_inputs(seed, part) draws one part's arguments, and reference() takes and returns one part's arrays. A program takes and returns all parts, laid end to end along the dimension named above; each array names one. Nothing has to cross between parts.
Inputs may be any that keep to these rules, and one draw needn't show every extreme that they name: `kept_blocks`: row b lists 8 distinct key blocks in increasing order; b itself is one of them, and for every listed block j the difference j // 2 - b // 2 is 0 or plus or minus a power of two of at most 8.
All inputs are finite; a program needn't handle non-finite values.
Results may differ from the reference program's by a relative error of at most 0.0065.
Values may be sent and summed in bfloat16 or wider, within the bound.
No kernel may reach another device: no remote copies, remote signals or barrier semaphores. Data moves between devices by JAX's collectives and lax.ppermute only.
A program may use at most 128 MiB of HBM per device.

```python
import math
import jax
import jax.numpy as jnp
from jax import lax

H = 20
DH = 128
BLOCK = 128
BD = 2
KEEP = 8
REACH = 8
NB = 32
SEQ = 4096


def draw_queries(key, part):
    values_drawn = jnp.clip(jax.random.normal(jax.random.fold_in(key, 1), (SEQ, H * DH), jnp.float32), -4.0, 4.0)
    return values_drawn.astype(jnp.bfloat16)


def draw_keys(key, part):
    values_drawn = jnp.clip(jax.random.normal(jax.random.fold_in(key, 2), (SEQ, H * DH), jnp.float32), -4.0, 4.0)
    return values_drawn.astype(jnp.bfloat16)


def draw_kept_blocks(key, part):
    blocks = jnp.arange(NB, dtype=jnp.int32)
    owner_device = blocks // BD
    offsets = [0]
    distance = 1
    farthest = min(REACH, NB // BD - 1)
    while distance <= farthest:
        offsets = offsets + [distance, -distance]
        distance = distance * 2
    columns = []
    for offset in offsets:
        for within in range(BD):
            columns.append((owner_device + offset) * BD + within)
    candidates = jnp.stack(columns, axis=1).astype(jnp.int32)
    candidate_count = candidates.shape[1]
    usable = (candidates >= 0) & (candidates < NB) & (candidates != blocks[:, None])
    random_rank = jax.random.randint(jax.random.fold_in(key, 7), (NB, candidate_count), 0, 4096, dtype=jnp.int32)
    ranking = jnp.where(usable, random_rank * candidate_count + jnp.arange(candidate_count, dtype=jnp.int32)[None, :], -1)
    ranked, picked = lax.top_k(ranking, KEEP - 1)
    chosen = jnp.take_along_axis(candidates, picked, axis=1)
    return jnp.sort(jnp.concatenate([blocks[:, None], chosen], axis=1), axis=1).astype(jnp.int32)


def shard_levels(rng, extent, shards, low, largest):
    loudness = 1.0
    for dim, blocks in shards:
        steps = jax.random.uniform(jax.random.fold_in(jax.random.fold_in(rng, 6), dim), (blocks,), jnp.float32, low / len(shards), largest / len(shards))
        loudness = loudness * jnp.repeat(jnp.exp(steps), extent[dim] // blocks).reshape((-1,) + (1,) * (len(extent) - 1 - dim))
    return loudness


def scatter_about(rng, dims, spread, bound, shards=(), held_as=jnp.bfloat16):
    array = spread * jax.random.normal(rng, dims, jnp.float32)
    if shards:
        array = array * shard_levels(rng, dims, shards, -0.22, 0.18)
    return jnp.clip(array, -bound, bound).astype(held_as)


def setup_inputs(seed: int = 0, part: int = 0) -> dict:
    key_list = jax.random.split(jax.random.key(seed), 5)
    part_splits = jax.random.split(jax.random.fold_in(key_list[4], part), 5)
    queries = draw_queries(jax.random.fold_in(jax.random.fold_in(key_list[4], part), 71), part)
    keys = draw_keys(jax.random.fold_in(jax.random.fold_in(key_list[4], part), 71), part)
    values = scatter_about(part_splits[2], (SEQ, H * DH), 1.0, 6.0, ((0, 16),))
    kept_blocks = draw_kept_blocks(jax.random.fold_in(jax.random.fold_in(key_list[4], part), 71), part)
    return dict(queries=queries, keys=keys, values=values, kept_blocks=kept_blocks)


def reference(queries, keys, values, kept_blocks):
    query_all = queries.reshape(NB, BLOCK, H, DH)
    key_all = keys.reshape(NB, BLOCK, H, DH)
    value_all = values.reshape(NB, BLOCK, H, DH)
    scale_factor = 1.0 / math.sqrt(DH)

    def attend_block(block_number):
        listed = kept_blocks[block_number].astype(jnp.int32)
        query_rows = query_all[block_number].astype(jnp.float32)
        key_rows = key_all[listed].reshape(KEEP * BLOCK, H, DH).astype(jnp.float32)
        value_rows = value_all[listed].reshape(KEEP * BLOCK, H, DH).astype(jnp.float32)
        scores = jnp.einsum('qhd,khd->hqk', query_rows, key_rows) * scale_factor
        top = lax.optimization_barrier(jnp.max(scores, axis=-1))
        weight = jnp.exp(scores - top[..., None])
        total = lax.optimization_barrier(jnp.sum(weight, axis=-1))
        rounded = lax.optimization_barrier(weight.astype(jnp.bfloat16)).astype(jnp.float32)
        numerator = jnp.einsum('hqk,khd->qhd', rounded, value_rows)
        result = numerator / jnp.transpose(total)[:, :, None]
        return result.astype(jnp.bfloat16)
    outputs = lax.map(attend_block, jnp.arange(NB, dtype=jnp.int32))
    return outputs.reshape(SEQ, H * DH)
```

```python
import functools
import math

import jax
import jax.numpy as jnp
from jax import lax
from jax.experimental import pallas as pl
from jax.experimental.pallas import tpu as pltpu
from jax.sharding import PartitionSpec as P

DH = 128
BLOCK = 128
HEAD_SPLIT = (5, 5, 5, 5)
TILES = 9


def head_chunks(heads):
    chunks, first = [], 0
    for count in HEAD_SPLIT:
        count = min(count, heads - first)
        if count > 0:
            chunks.append((first, count))
            first += count
    if first < heads:
        chunks.append((first, heads - first))
    return chunks


def shifted(value, steps):
    count = lax.axis_size("blk")
    pairs = [(i, i + steps) for i in range(count) if 0 <= i + steps < count]
    return lax.ppermute(value, "blk", pairs)


def swapped(value, bit):
    count = lax.axis_size("blk")
    return lax.ppermute(value, "blk", [(i, i ^ bit) for i in range(count)])


def attend_kernel(first, count, local_blocks, keep, place, kept, *refs):
    q_hbm, k_hbm, v_hbm = refs[:3]
    remote = refs[3 : 3 + TILES - 1]
    out_hbm = refs[3 + TILES]
    queries, tiles, result, sems, out_sem = refs[4 + TILES :]
    columns = pl.ds(first * DH, count * DH)
    copies = [
        pltpu.make_async_copy(q_hbm.at[:, columns], queries, sems.at[0]),
        pltpu.make_async_copy(k_hbm.at[:, columns], tiles.at[0, 0], sems.at[1]),
        pltpu.make_async_copy(v_hbm.at[:, columns], tiles.at[0, 1], sems.at[2]),
    ]
    for index, ref in enumerate(remote):
        copies.append(pltpu.make_async_copy(ref, tiles.at[index + 1], sems.at[3 + index]))
    for copy in copies:
        copy.start()
    for copy in copies:
        copy.wait()
    position = place[0]
    core, side = position % 2, (position // 2) % 2
    scale = math.log2(math.e) / math.sqrt(DH)
    for block in range(local_blocks):
        slots, halves = [], []
        for entry in range(keep):
            listed = kept[block, entry]
            offset = listed // local_blocks - position
            ahead = (offset > 0).astype(jnp.int32)
            near = jnp.abs(offset)
            step = (
                (near >= 1).astype(jnp.int32)
                + (near >= 2).astype(jnp.int32)
                + (near >= 4).astype(jnp.int32)
                + (near >= 8).astype(jnp.int32)
            )
            flip = jnp.where(step == 1, core, jnp.where(step == 2, side, 0))
            first_of_pair = (ahead + flip) % 2
            slots.append(jnp.where(step == 0, 0, 2 * step - first_of_pair))
            halves.append(pl.multiple_of((listed % local_blocks) * BLOCK, BLOCK))
        for head in range(count):
            lanes = pl.ds(head * DH, DH)
            query = queries[pl.ds(block * BLOCK, BLOCK), lanes]
            keys = jnp.concatenate(
                [tiles[s, 0, pl.ds(h, BLOCK), lanes] for s, h in zip(slots, halves)], axis=0
            )
            values = jnp.concatenate(
                [tiles[s, 1, pl.ds(h, BLOCK), lanes] for s, h in zip(slots, halves)], axis=0
            )
            scores = lax.dot_general(
                query, keys, (((1,), (1,)), ((), ())), preferred_element_type=jnp.float32
            )
            top = jnp.max(scores, axis=1, keepdims=True)
            weight = jnp.exp2((scores - top) * scale)
            total = jnp.sum(weight, axis=1, keepdims=True)
            numerator = jnp.dot(
                weight.astype(jnp.bfloat16), values, preferred_element_type=jnp.float32
            )
            result[pl.ds(block * BLOCK, BLOCK), lanes] = (numerator / total).astype(jnp.bfloat16)
    copy = pltpu.make_async_copy(result, out_hbm.at[:, columns], out_sem)
    copy.start()
    copy.wait()


def attend(first, count, place, kept, queries, keys, values, remote, attended):
    rows = queries.shape[0]
    local_blocks, keep = kept.shape
    width = count * DH
    anywhere = pl.BlockSpec(memory_space=pl.ANY)
    scalars = pl.BlockSpec(memory_space=pltpu.SMEM)
    pairs = local_blocks * keep * count
    return pl.pallas_call(
        functools.partial(attend_kernel, first, count, local_blocks, keep),
        out_shape=jax.ShapeDtypeStruct(attended.shape, attended.dtype),
        in_specs=[scalars, scalars] + [anywhere] * (3 + len(remote) + 1),
        out_specs=anywhere,
        scratch_shapes=[
            pltpu.VMEM((rows, width), jnp.bfloat16),
            pltpu.VMEM((TILES, 2, rows, width), jnp.bfloat16),
            pltpu.VMEM((rows, width), jnp.bfloat16),
            pltpu.SemaphoreType.DMA((2 + TILES,)),
            pltpu.SemaphoreType.DMA,
        ],
        input_output_aliases={5 + len(remote): 0},
        compiler_params=pltpu.CompilerParams(vmem_limit_bytes=40 * 1024 * 1024),
        cost_estimate=pl.CostEstimate(
            flops=4 * pairs * BLOCK * BLOCK * DH,
            bytes_accessed=(2 * TILES + 2) * rows * width * 2,
            transcendentals=pairs * BLOCK * BLOCK,
        ),
        name=f"attend_{first}",
    )(place, kept, queries, keys, values, *remote, attended)


def per_device(queries, keys, values, kept_blocks):
    position = lax.axis_index("blk")
    place = position.astype(jnp.int32).reshape(1)
    core, side = position % 2, (position // 2) % 2
    heads = queries.shape[1] // DH
    chunks = head_chunks(heads)
    own = []
    for first, count in chunks:
        lanes = slice(first * DH, (first + count) * DH)
        own.append(jnp.stack((keys[:, lanes], values[:, lanes])))
    attended = jnp.zeros(queries.shape, jnp.bfloat16)
    for (first, count), tile in zip(chunks, own):
        from_below, from_above = shifted(tile, 4), shifted(tile, -4)
        near_side = swapped(tile, 2)
        near_core = swapped(tile, 1)
        far_below, far_above = shifted(from_below, 4), shifted(from_above, -4)
        far_side = swapped(jnp.where(side == 0, from_above, from_below), 2)
        far_core = swapped(jnp.where(core == side, near_side, far_side), 1)
        remote = (
            near_core, far_core, near_side, far_side, from_above, from_below, far_above, far_below
        )
        attended = attend(
            first, count, place, kept_blocks, queries, keys, values, remote, attended
        )
    return attended


def solution(mesh):
    placed = P(("clip", "blk"), None)
    return jax.shard_map(
        per_device, mesh=mesh, in_specs=(placed,) * 4, out_specs=placed, check_vma=False
    )
```

```python
import functools
import math

import jax
import jax.numpy as jnp
from jax import lax
from jax.experimental import pallas as pl
from jax.experimental.pallas import tpu as pltpu
from jax.sharding import PartitionSpec as P

DH = 128
BLOCK = 128
VALUE_SPLIT = (20,)
VMEM = 18 * 1024 * 1024


def permuted(value, target):
    count = lax.axis_size("blk")
    pairs = [(i, target(i)) for i in range(count)]
    return lax.ppermute(value, "blk", [(i, t) for i, t in pairs if t is not None and 0 <= t < count])


def swapped(value, bit):
    return permuted(value, lambda i: i ^ bit)


def swapped_odd(value):
    return permuted(value, lambda i: i + 4 if i & 4 else i - 4)


def far_even(value):
    count = lax.axis_size("blk")
    return permuted(value, lambda i: i ^ 4 if 0 <= (i + 4 if i & 4 else i - 4) < count else None)


def far_side(value):
    count = lax.axis_size("blk")
    return permuted(value, lambda i: i ^ 2 if 0 <= (i - 4 if i & 2 else i + 4) < count else None)


def after(value, *earlier):
    return lax.optimization_barrier((value, *earlier))[0]


def slots_of(place, kept, block, local_blocks, keep):
    position = place[0]
    bits = [position % 2, (position // 2) % 2, (position // 4) % 2]
    found = []
    for entry in range(keep):
        listed = kept[block, entry]
        offset = listed // local_blocks - position
        ahead = (offset > 0).astype(jnp.int32)
        near = jnp.abs(offset)
        step = sum((near >= reach).astype(jnp.int32) for reach in (1, 2, 4, 8))
        flip = jnp.where(step == 1, bits[0], jnp.where(step == 2, bits[1], bits[2]))
        slot = jnp.where(step == 0, 0, 2 * step - (ahead + flip) % 2)
        found.append((slot, pl.multiple_of((listed % local_blocks) * BLOCK, BLOCK)))
    return found


def score_kernel(local_blocks, keep, place, kept, queries, *refs):
    tiles, (weights, totals), staged = refs[:9], refs[9:11], refs[11]
    scale = math.log2(math.e) / math.sqrt(DH)
    found = [slots_of(place, kept, block, local_blocks, keep) for block in range(local_blocks)]

    def one_head(head, carry):
        lanes = pl.ds(pl.multiple_of(head * DH, DH), DH)
        for index, tile in enumerate(tiles):
            staged[index] = tile[:, lanes]
        for block in range(local_blocks):
            rows = pl.ds(block * BLOCK, BLOCK)
            keys = jnp.concatenate(
                [staged[slot, pl.ds(row, BLOCK), :] for slot, row in found[block]], axis=0
            )
            scores = lax.dot_general(
                queries[rows, lanes],
                keys,
                (((1,), (1,)), ((), ())),
                preferred_element_type=jnp.float32,
            )
            top = jnp.max(scores, axis=1, keepdims=True)
            weight = jnp.exp2((scores - top) * scale)
            total = jnp.sum(weight, axis=1, keepdims=True)
            weights[head, rows, :] = weight.astype(jnp.bfloat16)
            totals[head, rows, :] = jnp.broadcast_to(total, (BLOCK, DH))
        return carry

    lax.fori_loop(0, queries.shape[1] // DH, one_head, 0, unroll=2)


def value_kernel(first, count, local_blocks, keep, place, kept, weights, totals, *refs):
    tiles, attended, staged = refs[:9], refs[9], refs[10]
    found = [slots_of(place, kept, block, local_blocks, keep) for block in range(local_blocks)]

    def one_head(head, carry):
        part = pl.ds(pl.multiple_of(head * DH, DH), DH)
        whole = pl.ds(pl.multiple_of((first + head) * DH, DH), DH)
        for index, tile in enumerate(tiles):
            staged[index] = tile[:, part if tile.shape[1] == count * DH else whole]
        for block in range(local_blocks):
            rows = pl.ds(block * BLOCK, BLOCK)
            values = jnp.concatenate(
                [staged[slot, pl.ds(row, BLOCK), :] for slot, row in found[block]], axis=0
            )
            numerator = jnp.dot(
                weights[first + head, rows, :], values, preferred_element_type=jnp.float32
            )
            attended[rows, part] = (numerator / totals[first + head, rows, :]).astype(jnp.bfloat16)
        return carry

    lax.fori_loop(0, count, one_head, 0, unroll=2)


def in_vmem(arrays):
    return [pltpu.with_memory_space_constraint(array, pltpu.VMEM) for array in arrays]


def weigh(place, kept, queries, tiles):
    rows, columns = queries.shape
    heads = columns // DH
    local_blocks, keep = kept.shape
    scalars = pl.BlockSpec(memory_space=pltpu.SMEM)
    held = pl.BlockSpec(memory_space=pltpu.VMEM)
    pairs = local_blocks * keep * heads
    return pl.pallas_call(
        functools.partial(score_kernel, local_blocks, keep),
        out_shape=(
            pltpu.VMEM((heads, rows, keep * BLOCK), jnp.bfloat16),
            pltpu.VMEM((heads, rows, DH), jnp.float32),
        ),
        in_specs=[scalars, scalars] + [held] * (1 + len(tiles)),
        out_specs=(held, held),
        scratch_shapes=[pltpu.VMEM((len(tiles), rows, DH), jnp.bfloat16)],
        compiler_params=pltpu.CompilerParams(vmem_limit_bytes=VMEM),
        cost_estimate=pl.CostEstimate(
            flops=2 * pairs * BLOCK * BLOCK * DH,
            bytes_accessed=(len(tiles) + 1) * rows * columns * 2 + heads * rows * keep * BLOCK * 2,
            transcendentals=pairs * BLOCK * BLOCK,
        ),
        name="weigh",
    )(place, kept, *in_vmem((queries, *tiles)))


def combine(first, count, place, kept, weights, totals, tiles):
    heads, rows, _ = weights.shape
    local_blocks, keep = kept.shape
    scalars = pl.BlockSpec(memory_space=pltpu.SMEM)
    held = pl.BlockSpec(memory_space=pltpu.VMEM)
    return pl.pallas_call(
        functools.partial(value_kernel, first, count, local_blocks, keep),
        out_shape=jax.ShapeDtypeStruct((rows, count * DH), jnp.bfloat16),
        in_specs=[scalars, scalars] + [held] * (2 + len(tiles)),
        out_specs=held,
        scratch_shapes=[pltpu.VMEM((len(tiles), rows, DH), jnp.bfloat16)],
        compiler_params=pltpu.CompilerParams(vmem_limit_bytes=VMEM),
        cost_estimate=pl.CostEstimate(
            flops=2 * local_blocks * keep * count * BLOCK * BLOCK * DH,
            bytes_accessed=len(tiles) * rows * count * DH * 2 + count * rows * keep * BLOCK * 2,
            transcendentals=0,
        ),
        name=f"combine_{first}",
    )(place, kept, *in_vmem((weights, totals, *tiles)))


def per_device(queries, keys, values, kept_blocks):
    position = lax.axis_index("blk").astype(jnp.int32)
    place = position.reshape(1)
    core_bit, side_bit, level_bit = (position % 2, (position // 2) % 2, (position // 4) % 2)
    same_side, same_core = side_bit == level_bit, core_bit == side_bit
    heads = queries.shape[1] // DH

    k_side, k_odd, k_even = swapped(keys, 2), swapped_odd(keys), swapped(keys, 4)
    v_side, v_odd, v_even = swapped(after(values, k_side), 2), swapped_odd(values), swapped(values, 4)
    k_mix = jnp.where(same_side, k_even, k_odd)
    k_odd_far, k_even_far = swapped_odd(k_even), far_even(k_odd)
    k_side_far = far_side(after(k_mix, v_side))
    v_mix = jnp.where(same_side, after(v_even, v_side), after(v_odd, v_side))
    k_core = swapped(after(keys, v_odd, v_even, v_mix), 1)
    v_core = swapped(after(values, v_odd, v_even, v_mix), 1)
    v_odd_far = swapped_odd(after(v_even, v_side))
    v_even_far = far_even(after(v_odd, v_side))
    v_side_far = far_side(after(v_mix, k_side_far))
    k_core_far = swapped(after(jnp.where(same_core, k_side, k_side_far), k_core, v_core, k_odd_far, k_even_far), 1)

    tiles = (keys, k_core, k_core_far, k_side, k_side_far, k_even, k_odd, k_even_far, k_odd_far)
    weights, totals = weigh(place, kept_blocks, queries, tiles)

    v_side_done = after(v_side_far, totals)
    v_core_far = swapped(jnp.where(same_core, v_side, v_side_done), 1)
    tiles = (
        values, v_core, v_core_far, v_side, v_side_done, v_even, v_odd, v_even_far, v_odd_far
    )
    return combine(0, heads, place, kept_blocks, weights, totals, tiles)


def solution(mesh):
    placed = P(("clip", "blk"), None)
    return jax.shard_map(
        per_device, mesh=mesh, in_specs=(placed,) * 4, out_specs=placed, check_vma=False
    )
```

```python
import functools
import math

import jax
import jax.numpy as jnp
from jax import lax
from jax.experimental import pallas as pl
from jax.experimental.pallas import tpu as pltpu
from jax.sharding import PartitionSpec as P

DH = 128
BLOCK = 128
NEAR, FAR = (0, 1, 3, 5, 6), (2, 4, 7, 8)
TILES = 9
GROUPS = 4
UNROLL = 5


def permuted(value, target):
    count = lax.axis_size("blk")
    pairs = [(i, target(i)) for i in range(count)]
    return lax.ppermute(value, "blk", [(i, t) for i, t in pairs if t is not None and 0 <= t < count])


def swapped(value, bit):
    return permuted(value, lambda i: i ^ bit)


def swapped_odd(value):
    return permuted(value, lambda i: i + 4 if i & 4 else i - 4)


def far_even(value):
    count = lax.axis_size("blk")
    return permuted(value, lambda i: i ^ 4 if 0 <= (i + 4 if i & 4 else i - 4) < count else None)


def far_side(value):
    count = lax.axis_size("blk")
    return permuted(value, lambda i: i ^ 2 if 0 <= (i - 4 if i & 2 else i + 4) < count else None)


def after(value, *earlier):
    return lax.optimization_barrier((value, *earlier))[0]


def slots_of(place, kept, block, local_blocks, keep):
    position = place[0]
    bits = [position % 2, (position // 2) % 2, (position // 4) % 2]
    found = []
    for entry in range(keep):
        listed = kept[block, entry]
        offset = listed // local_blocks - position
        ahead = (offset > 0).astype(jnp.int32)
        near = jnp.abs(offset)
        step = sum((near >= reach).astype(jnp.int32) for reach in (1, 2, 4, 8))
        flip = jnp.where(step == 1, bits[0], jnp.where(step == 2, bits[1], bits[2]))
        slot = jnp.where(step == 0, 0, 2 * step - (ahead + flip) % 2)
        found.append((slot, pl.multiple_of((listed % local_blocks) * BLOCK, BLOCK)))
    return found


def score_kernel(local_blocks, keep, groups, place, kept, queries, *refs):
    tiles, near = refs[:TILES], refs[TILES : TILES + len(NEAR)]
    weights, totals, values, keys, key_sems, value_sems = refs[TILES + len(NEAR) :]
    copies = []
    for group, (first, count) in enumerate(groups):
        lanes = pl.ds(first * DH, count * DH)
        copies.append(
            [
                pltpu.make_async_copy(
                    tile.at[:, lanes], keys.at[index, :, lanes], key_sems.at[group, index]
                )
                for index, tile in enumerate(tiles)
            ]
        )
        for copy in copies[-1]:
            copy.start()
    value_copies = [
        pltpu.make_async_copy(tile, values.at[slot], value_sems.at[index])
        for index, (slot, tile) in enumerate(zip(NEAR, near))
    ]
    for copy in value_copies:
        copy.start()
    scale = math.log2(math.e) / math.sqrt(DH)
    found = [slots_of(place, kept, block, local_blocks, keep) for block in range(local_blocks)]

    def one_head(head, carry):
        lanes = pl.ds(pl.multiple_of(head * DH, DH), DH)
        for block in range(local_blocks):
            rows = pl.ds(block * BLOCK, BLOCK)
            gathered = jnp.concatenate(
                [keys[slot, pl.ds(row, BLOCK), lanes] for slot, row in found[block]], axis=0
            )
            scores = lax.dot_general(
                queries[rows, lanes],
                gathered,
                (((1,), (1,)), ((), ())),
                preferred_element_type=jnp.float32,
            )
            top = jnp.max(scores, axis=1, keepdims=True)
            weight = jnp.exp2((scores - top) * scale)
            total = jnp.sum(weight, axis=1, keepdims=True)
            weights[head, rows, :] = weight.astype(jnp.bfloat16)
            totals[head, rows, :] = jnp.broadcast_to(total, (BLOCK, DH))
        return carry

    for (first, count), arriving in zip(groups, copies):
        for copy in arriving:
            copy.wait()
        lax.fori_loop(first, first + count, one_head, 0, unroll=UNROLL)
    for copy in value_copies:
        copy.wait()


def value_kernel(local_blocks, keep, groups, place, kept, weights, totals, *refs):
    far, (attended, values, result, far_sems, out_sems) = refs[1:-5], refs[-5:]
    copies = []
    for group, (first, count) in enumerate(groups):
        lanes = pl.ds(first * DH, count * DH)
        arriving = []
        for index, (slot, tile) in enumerate(zip(FAR, far)):
            arriving.append(
                pltpu.make_async_copy(
                    tile.at[:, lanes], values.at[slot, :, lanes], far_sems.at[group, index]
                )
            )
        for copy in arriving:
            copy.start()
        copies.append(arriving)
    found = [slots_of(place, kept, block, local_blocks, keep) for block in range(local_blocks)]

    def one_head(head, carry):
        lanes = pl.ds(pl.multiple_of(head * DH, DH), DH)
        for block in range(local_blocks):
            rows = pl.ds(block * BLOCK, BLOCK)
            gathered = jnp.concatenate(
                [values[slot, pl.ds(row, BLOCK), lanes] for slot, row in found[block]], axis=0
            )
            numerator = jnp.dot(
                weights[head, rows, :], gathered, preferred_element_type=jnp.float32
            )
            result[rows, lanes] = (numerator / totals[head, rows, :]).astype(jnp.bfloat16)
        return carry

    leaving = []
    for group, (first, count) in enumerate(groups):
        for copy in copies[group]:
            copy.wait()
        lax.fori_loop(first, first + count, one_head, 0, unroll=UNROLL)
        lanes = pl.ds(first * DH, count * DH)
        leaving.append(
            pltpu.make_async_copy(
                result.at[:, lanes], attended.at[:, lanes], out_sems.at[group]
            )
        )
        leaving[-1].start()
    for copy in leaving:
        copy.wait()


def in_vmem(array):
    return pltpu.with_memory_space_constraint(array, pltpu.VMEM)


def weigh(place, kept, queries, tiles, near, groups):
    rows, columns = queries.shape
    heads = columns // DH
    local_blocks, keep = kept.shape
    scalars = pl.BlockSpec(memory_space=pltpu.SMEM)
    held = pl.BlockSpec(memory_space=pltpu.VMEM)
    anywhere = pl.BlockSpec(memory_space=pl.ANY)
    pairs = local_blocks * keep * heads
    return pl.pallas_call(
        functools.partial(score_kernel, local_blocks, keep, groups),
        out_shape=(
            pltpu.VMEM((heads, rows, keep * BLOCK), jnp.bfloat16),
            pltpu.VMEM((heads, rows, DH), jnp.float32),
            pltpu.VMEM((TILES, rows, columns), jnp.bfloat16),
        ),
        in_specs=[scalars, scalars, held] + [anywhere] * (len(tiles) + len(near)),
        out_specs=(held, held, held),
        scratch_shapes=[
            pltpu.VMEM((TILES, rows, columns), jnp.bfloat16),
            pltpu.SemaphoreType.DMA((len(groups), TILES)),
            pltpu.SemaphoreType.DMA((len(near),)),
        ],
        compiler_params=pltpu.CompilerParams(vmem_limit_bytes=16 * 1024 * 1024),
        cost_estimate=pl.CostEstimate(
            flops=2 * pairs * BLOCK * BLOCK * DH,
            bytes_accessed=(len(tiles) + 1) * rows * columns * 2 + heads * rows * keep * BLOCK * 2,
            transcendentals=pairs * BLOCK * BLOCK,
        ),
        name="weigh",
    )(place, kept, in_vmem(queries), *tiles, *near)


def combine(place, kept, weights, totals, values, far, groups):
    heads, rows, _ = weights.shape
    local_blocks, keep = kept.shape
    scalars = pl.BlockSpec(memory_space=pltpu.SMEM)
    held = pl.BlockSpec(memory_space=pltpu.VMEM)
    anywhere = pl.BlockSpec(memory_space=pl.ANY)
    return pl.pallas_call(
        functools.partial(value_kernel, local_blocks, keep, groups),
        out_shape=(
            jax.ShapeDtypeStruct((rows, heads * DH), jnp.bfloat16),
            pltpu.VMEM(values.shape, values.dtype),
        ),
        in_specs=[scalars, scalars] + [held] * 3 + [anywhere] * len(far),
        out_specs=(anywhere, held),
        input_output_aliases={4: 1},
        scratch_shapes=[
            pltpu.VMEM((rows, heads * DH), jnp.bfloat16),
            pltpu.SemaphoreType.DMA((len(groups), len(FAR))),
            pltpu.SemaphoreType.DMA((len(groups),)),
        ],
        compiler_params=pltpu.CompilerParams(vmem_limit_bytes=4 * 1024 * 1024),
        cost_estimate=pl.CostEstimate(
            flops=2 * local_blocks * keep * heads * BLOCK * BLOCK * DH,
            bytes_accessed=len(FAR) * rows * heads * DH * 2,
            transcendentals=0,
        ),
        name="combine",
    )(place, kept, in_vmem(weights), in_vmem(totals), in_vmem(values), *far)[0]


def per_device(queries, keys, values, kept_blocks):
    position = lax.axis_index("blk").astype(jnp.int32)
    place = position.reshape(1)
    core_bit, side_bit, level_bit = (position % 2, (position // 2) % 2, (position // 4) % 2)
    same_side, same_core = side_bit == level_bit, core_bit == side_bit
    heads = queries.shape[1] // DH

    count = heads // GROUPS
    groups = [(first, count) for first in range(0, heads, count)]

    k_side, k_odd, k_even = swapped(keys, 2), swapped_odd(keys), swapped(keys, 4)
    v_side, v_odd, v_even = swapped(after(values, k_side), 2), swapped_odd(values), swapped(values, 4)
    k_mix = jnp.where(same_side, k_even, k_odd)
    k_odd_far, k_even_far = swapped_odd(k_even), swapped(k_odd, 4)
    k_side_far = swapped(after(k_mix, v_side), 2)
    v_mix = jnp.where(same_side, after(v_even, v_side), after(v_odd, v_side))
    k_core = swapped(after(keys, v_odd, v_even, v_mix), 1)
    v_core = swapped(after(values, v_odd, v_even, v_mix), 1)
    v_odd_far = swapped_odd(after(v_even, v_side))
    v_even_far = swapped(after(v_odd, v_side), 4)
    v_side_far = swapped(after(v_mix, k_side_far), 2)
    k_core_far = swapped(
        after(jnp.where(same_core, k_side, k_side_far), k_core, v_core, k_odd_far, k_even_far), 1
    )

    tiles = (keys, k_core, k_core_far, k_side, k_side_far, k_even, k_odd, k_even_far, k_odd_far)
    near = (values, v_core, v_side, v_even, v_odd)
    weights, totals, staged = weigh(place, kept_blocks, queries, tiles, near, groups)

    v_side_done = after(v_side_far, totals)
    v_core_far = swapped(jnp.where(same_core, v_side, v_side_done), 1)
    far = (v_core_far, v_side_done, v_even_far, v_odd_far)
    return combine(place, kept_blocks, weights, totals, staged, far, groups)


def solution(mesh):
    placed = P(("clip", "blk"), None)
    return jax.shard_map(
        per_device, mesh=mesh, in_specs=(placed,) * 4, out_specs=placed, check_vma=False
    )
```

```python
import functools
import math

import jax
import jax.numpy as jnp
from jax import lax
from jax.experimental import pallas as pl
from jax.experimental.pallas import tpu as pltpu
from jax.sharding import PartitionSpec as P

DH = 128
BLOCK = 128
LANES = 128
VALUE_SPLIT = (15, 5)
GROUP = 5
OWN_TILES = 6
FAR = (4, 5)
LENT_TILES = 4
SCALE = math.log2(math.e) / math.sqrt(DH)
MASKED = -1e30


def permuted(value, target):
    count = lax.axis_size("blk")
    pairs = [(i, target(i)) for i in range(count)]
    return lax.ppermute(value, "blk", [(i, t) for i, t in pairs if 0 <= t < count])


def swapped(value, bit):
    return permuted(value, lambda i: i ^ bit)


def swapped_odd(value):
    return permuted(value, lambda i: i + 4 if i & 4 else i - 4)


def after(value, *earlier):
    return lax.optimization_barrier((value, *earlier))[0]


def number(flag):
    return flag.astype(jnp.int32)


def own_entries(place, kept, block, local_blocks, keep):
    position = place[0]
    pair = position + 1 - 2 * (position % 2)
    level = (position // 4) % 2
    found = []
    for entry in range(keep):
        listed = kept[block, entry]
        device = listed // local_blocks
        offset = device - position
        near = jnp.abs(offset)
        side = 1 - (number(offset > 0) + level) % 2
        slot = jnp.where(near == 8, 4 + side, jnp.where(near == 4, 2 + side, number(device == pair)))
        lent = (near == 2) | ((near == 1) & (device != pair))
        slot = jnp.where(lent, 0, slot)
        bias = jnp.where(lent, jnp.float32(MASKED), jnp.float32(0))
        found.append((slot, pl.multiple_of((listed % local_blocks) * BLOCK, BLOCK), bias))
    return found


def lent_entries(place, kept, block, local_blocks, keep):
    position = place[0]
    client = position + 2 - 4 * ((position // 2) % 2)
    pair = position + 1 - 2 * (position % 2)
    client_pair = client + 1 - 2 * (client % 2)
    found = []
    for entry in range(keep):
        listed = kept[block, entry]
        device = listed // local_blocks
        near = jnp.abs(device - client)
        lent = (near == 2) | ((near == 1) & (device != client_pair))
        slot = jnp.where(near == 2, number(device != position), 2 + number(device != pair))
        slot = jnp.where(lent, slot, 0)
        bias = jnp.where(lent, jnp.float32(0), jnp.float32(MASKED))
        found.append((slot, pl.multiple_of((listed % local_blocks) * BLOCK, BLOCK), bias))
    return found


def weigh_block(query, keys, lanes, found):
    gathered = jnp.concatenate(
        [keys[slot, pl.ds(row, BLOCK), lanes] for slot, row, _ in found], axis=0
    )
    scores = lax.dot_general(
        query, gathered, (((1,), (1,)), ((), ())), preferred_element_type=jnp.float32
    )
    bias = jnp.concatenate([jnp.full((1, BLOCK), part, jnp.float32) for _, _, part in found], axis=1)
    scores = scores + bias
    top = jnp.max(scores, axis=1, keepdims=True)
    weight = jnp.exp2((scores - top) * SCALE)
    total = jnp.sum(weight, axis=1, keepdims=True)
    return top, total, weight.astype(jnp.bfloat16)


def sum_block(weight, values, lanes, found):
    gathered = jnp.concatenate(
        [values[slot, pl.ds(row, BLOCK), lanes] for slot, row, _ in found], axis=0
    )
    return jnp.dot(weight, gathered, preferred_element_type=jnp.float32)


def copied(sources, target, sems, lanes):
    copies = []
    for index, source in enumerate(sources):
        copies.append(
            pltpu.make_async_copy(source.at[:, lanes], target.at[index, :, lanes], sems.at[index])
        )
        copies[-1].start()
    return copies


def score_kernel(
    entries, local_blocks, keep, groups, tile_count, place, kept, queries, *refs
):
    key_tiles, near = refs[:tile_count], refs[tile_count:-6]
    weights, stats, values, keys, key_sems, value_sems = refs[-6:]
    copies = []
    for group, (first, count) in enumerate(groups):
        copies.append(copied(key_tiles, keys, key_sems.at[group], pl.ds(first * DH, count * DH)))
    value_copies = copied(near, values, value_sems, pl.ds(0, queries.shape[1]))
    found = [entries(place, kept, block, local_blocks, keep) for block in range(local_blocks)]
    for (first, count), arriving in zip(groups, copies):
        for copy in arriving:
            copy.wait()
        for head in range(first, first + count):
            lanes = pl.ds(head * DH, DH)
            for block in range(local_blocks):
                rows = pl.ds(block * BLOCK, BLOCK)
                top, total, weight = weigh_block(queries[rows, lanes], keys, lanes, found[block])
                weights[head, rows, :] = weight
                stats[0, rows, pl.ds(head, 1)] = top
                stats[1, rows, pl.ds(head, 1)] = total
    for copy in value_copies:
        copy.wait()


def lent_kernel(local_blocks, keep, groups, place, kept, weights, stats, *refs):
    tiles, (attended, values, sems) = refs[:LENT_TILES], refs[LENT_TILES:]
    copies = []
    for group, (first, count) in enumerate(groups):
        copies.append(copied(tiles, values, sems.at[group], pl.ds(first * DH, count * DH)))
    found = [lent_entries(place, kept, block, local_blocks, keep) for block in range(local_blocks)]
    shares = []
    for block in range(local_blocks):
        shares.append(1.0 / stats[1, pl.ds(block * BLOCK, BLOCK), :])
    for (first, count), arriving in zip(groups, copies):
        for copy in arriving:
            copy.wait()
        for head in range(first, first + count):
            lanes = pl.ds(head * DH, DH)
            for block in range(local_blocks):
                rows = pl.ds(block * BLOCK, BLOCK)
                numerator = sum_block(weights[head, rows, :], values, lanes, found[block])
                share = shares[block][:, head : head + 1]
                attended[rows, lanes] = (numerator * share).astype(jnp.bfloat16)


def value_kernel(local_blocks, keep, begin, groups, place, kept, weights, own, lent, *refs):
    borrowed, far = refs[1], refs[2 : 2 + len(FAR)]
    attended, values, result, far_sems, out_sems = refs[-5:]
    copies = []
    for group, (first, count) in enumerate(groups):
        lanes = pl.ds(first * DH, count * DH)
        part = pl.ds((first - begin) * DH, count * DH)
        copies.append([])
        for index, (slot, tile) in enumerate(zip(FAR, far)):
            copies[-1].append(
                pltpu.make_async_copy(
                    tile.at[:, part], values.at[slot, :, lanes], far_sems.at[group, index]
                )
            )
            copies[-1][-1].start()
    found = [own_entries(place, kept, block, local_blocks, keep) for block in range(local_blocks)]
    shares = []
    for block in range(local_blocks):
        rows = pl.ds(block * BLOCK, BLOCK)
        top = jnp.maximum(own[0, rows, :], lent[0, rows, :])
        own_scale = jnp.exp2((own[0, rows, :] - top) * SCALE)
        lent_total = lent[1, rows, :] * jnp.exp2((lent[0, rows, :] - top) * SCALE)
        total = own[1, rows, :] * own_scale + lent_total
        shares.append((own_scale / total, lent_total / total))
    leaving = []
    for group, (first, count) in enumerate(groups):
        for copy in copies[group]:
            copy.wait()
        for head in range(first, first + count):
            lanes = pl.ds(head * DH, DH)
            for block in range(local_blocks):
                rows = pl.ds(block * BLOCK, BLOCK)
                own_share, lent_share = (share[:, head : head + 1] for share in shares[block])
                numerator = sum_block(weights[head, rows, :], values, lanes, found[block])
                whole = numerator * own_share
                whole = whole + borrowed[rows, lanes].astype(jnp.float32) * lent_share
                result[rows, pl.ds((head - begin) * DH, DH)] = whole.astype(jnp.bfloat16)
        leaving.append(
            pltpu.make_async_copy(
                result.at[:, pl.ds((first - begin) * DH, count * DH)],
                attended.at[:, pl.ds(first * DH, count * DH)],
                out_sems.at[group],
            )
        )
        leaving[-1].start()
    for copy in leaving:
        copy.wait()


def in_vmem(arrays):
    return [pltpu.with_memory_space_constraint(array, pltpu.VMEM) for array in arrays]


def in_hbm(arrays):
    return [pltpu.with_memory_space_constraint(array, pltpu.HBM) for array in arrays]


SCALARS = pl.BlockSpec(memory_space=pltpu.SMEM)
HELD = pl.BlockSpec(memory_space=pltpu.VMEM)
ANYWHERE = pl.BlockSpec(memory_space=pl.ANY)


def cost(kept, heads, products, exponentials):
    pairs = kept.shape[0] * kept.shape[1] * heads * BLOCK * BLOCK
    return pl.CostEstimate(
        flops=2 * products * pairs * DH,
        bytes_accessed=2 * products * pairs,
        transcendentals=exponentials * pairs,
    )


def weigh(entries, place, kept, queries, tiles, near, stacked, groups, name):
    rows, columns = queries.shape
    heads = columns // DH
    return pl.pallas_call(
        functools.partial(score_kernel, entries, *kept.shape, groups, len(tiles)),
        out_shape=(
            pltpu.VMEM((heads, rows, kept.shape[1] * BLOCK), jnp.bfloat16),
            pltpu.VMEM((2, rows, LANES), jnp.float32),
            pltpu.VMEM((stacked, rows, columns), jnp.bfloat16),
        ),
        in_specs=[SCALARS, SCALARS, HELD] + [ANYWHERE] * (len(tiles) + len(near)),
        out_specs=(HELD, HELD, HELD),
        scratch_shapes=[
            pltpu.VMEM((len(tiles), rows, columns), jnp.bfloat16),
            pltpu.SemaphoreType.DMA((len(groups), len(tiles))),
            pltpu.SemaphoreType.DMA((max(1, len(near)),)),
        ],
        compiler_params=pltpu.CompilerParams(vmem_limit_bytes=14 * 1024 * 1024),
        cost_estimate=cost(kept, heads, 1, 1),
        name=name,
    )(place, kept, *in_vmem((queries,)), *in_hbm((*tiles, *near)))


def sum_lent(place, kept, weights, stats, tiles, groups):
    heads, rows, _ = weights.shape
    return pl.pallas_call(
        functools.partial(lent_kernel, *kept.shape, groups),
        out_shape=jax.ShapeDtypeStruct((rows, heads * DH), jnp.bfloat16),
        in_specs=[SCALARS, SCALARS, HELD, HELD] + [ANYWHERE] * LENT_TILES,
        out_specs=HELD,
        scratch_shapes=[
            pltpu.VMEM((LENT_TILES, rows, heads * DH), jnp.bfloat16),
            pltpu.SemaphoreType.DMA((len(groups), LENT_TILES)),
        ],
        compiler_params=pltpu.CompilerParams(vmem_limit_bytes=10 * 1024 * 1024),
        cost_estimate=cost(kept, heads, 1, 0),
        name="sum_lent",
    )(place, kept, *in_vmem((weights, stats)), *in_hbm(tiles))


def combine(place, kept, weights, own, lent, values, borrowed, far, begin, groups, before):
    heads, rows, _ = weights.shape
    operands = [place, kept, *in_vmem((weights, own, lent, values, borrowed)), *far]
    in_specs = [SCALARS, SCALARS] + [HELD] * 5 + [ANYWHERE] * len(far)
    aliases = {5: 1}
    if before is not None:
        aliases[len(operands)] = 0
        operands.append(before)
        in_specs.append(ANYWHERE)
    count = sum(count for _, count in groups)
    return pl.pallas_call(
        functools.partial(value_kernel, *kept.shape, begin, groups),
        out_shape=(
            jax.ShapeDtypeStruct((rows, heads * DH), jnp.bfloat16),
            pltpu.VMEM(values.shape, values.dtype),
        ),
        in_specs=in_specs,
        out_specs=(ANYWHERE, HELD),
        input_output_aliases=aliases,
        scratch_shapes=[
            pltpu.VMEM((rows, count * DH), jnp.bfloat16),
            pltpu.SemaphoreType.DMA((len(groups), len(FAR))),
            pltpu.SemaphoreType.DMA((len(groups),)),
        ],
        compiler_params=pltpu.CompilerParams(vmem_limit_bytes=6 * 1024 * 1024),
        cost_estimate=cost(kept, count, 1, 0),
        name=f"combine_{begin}",
    )(*operands)


def grouped(begin, count, size):
    return [(first, min(size, begin + count - first)) for first in range(begin, begin + count, size)]


def per_device(queries, keys, values, kept):
    position = lax.axis_index("blk").astype(jnp.int32)
    place = position.reshape(1)
    same_side = (position // 2) % 2 == (position // 4) % 2
    heads = queries.shape[1] // DH
    groups = grouped(0, heads, GROUP)

    k_odd, k_even = swapped_odd(keys), swapped(keys, 4)
    asked, asked_kept = swapped(queries, 2), swapped(kept, 2)
    later = after(values, asked_kept)
    v_odd, v_even = swapped_odd(later), swapped(later, 4)
    k_odd_far, k_even_far = swapped_odd(k_even), swapped(k_odd, 4)
    k_level = jnp.where(same_side, k_even, k_odd)
    v_level = jnp.where(same_side, v_even, v_odd)
    k_pair, k_pair_level = swapped(after(keys, k_level), 1), swapped(k_level, 1)
    v_pair, v_pair_level = swapped(after(values, v_level), 1), swapped(v_level, 1)
    lent_weights, lent_stats, _ = weigh(
        lent_entries, place, asked_kept, asked, (keys, k_level, k_pair, k_pair_level), (), 1,
        groups, "weigh_lent",
    )
    lent = swapped(lent_stats, 2)
    answer = sum_lent(
        place, asked_kept, lent_weights, lent_stats, (values, v_level, v_pair, v_pair_level), groups
    )
    borrowed = swapped(after(answer, lent), 2)
    weights, own, staged = weigh(
        own_entries, place, kept, after(queries, answer),
        (keys, k_pair, k_even, k_odd, k_even_far, k_odd_far),
        (values, v_pair, v_even, v_odd), OWN_TILES, groups, "weigh_own",
    )
    attended, begin, hold = None, 0, lent
    hops = []
    for count in VALUE_SPLIT:
        lanes = slice(begin * DH, (begin + count) * DH)
        hops.append(
            (swapped(after(v_odd[:, lanes], hold), 4), swapped_odd(after(v_even[:, lanes], hold)))
        )
        begin, hold = begin + count, own
    begin = 0
    for count, far in zip(VALUE_SPLIT, hops):
        attended, staged = combine(
            place, kept, weights, own, lent, staged, borrowed, far,
            begin, grouped(begin, count, GROUP), attended,
        )
        begin += count
    return attended


def solution(mesh):
    placed = P(("clip", "blk"), None)
    return jax.shard_map(
        per_device, mesh=mesh, in_specs=(placed,) * 4, out_specs=placed, check_vma=False
    )
```

```python
import functools
import math

import jax
import jax.numpy as jnp
from jax import lax
from jax.experimental import pallas as pl
from jax.experimental.pallas import tpu as pltpu
from jax.sharding import PartitionSpec as P

DH = 128
BLOCK = 128
LANES = 128
VALUE_SPLIT = (15, 5)
GROUP = 5
OWN_TILES = 6
FAR = (4, 5)
LENT_TILES = 4
SCALE = math.log2(math.e) / math.sqrt(DH)
MASKED = -1e30


def permuted(value, target):
    count = lax.axis_size("blk")
    pairs = [(i, target(i)) for i in range(count)]
    return lax.ppermute(value, "blk", [(i, t) for i, t in pairs if 0 <= t < count])


def swapped(value, bit):
    return permuted(value, lambda i: i ^ bit)


def swapped_odd(value):
    return permuted(value, lambda i: i + 4 if i & 4 else i - 4)


def after(value, *earlier):
    return lax.optimization_barrier((value, *earlier))[0]


def number(flag):
    return flag.astype(jnp.int32)


def own_entries(place, kept, block, local_blocks, keep):
    position = place[0]
    pair = position + 1 - 2 * (position % 2)
    level = (position // 4) % 2
    found = []
    for entry in range(keep):
        listed = kept[block, entry]
        device = listed // local_blocks
        offset = device - position
        near = jnp.abs(offset)
        side = 1 - (number(offset > 0) + level) % 2
        slot = jnp.where(near == 8, 4 + side, jnp.where(near == 4, 2 + side, number(device == pair)))
        lent = (near == 2) | ((near == 1) & (device != pair))
        slot = jnp.where(lent, 0, slot)
        bias = jnp.where(lent, jnp.float32(MASKED), jnp.float32(0))
        found.append((slot, pl.multiple_of((listed % local_blocks) * BLOCK, BLOCK), bias))
    return found


def lent_entries(place, kept, block, local_blocks, keep):
    position = place[0]
    client = position + 2 - 4 * ((position // 2) % 2)
    pair = position + 1 - 2 * (position % 2)
    client_pair = client + 1 - 2 * (client % 2)
    found = []
    for entry in range(keep):
        listed = kept[block, entry]
        device = listed // local_blocks
        near = jnp.abs(device - client)
        lent = (near == 2) | ((near == 1) & (device != client_pair))
        slot = jnp.where(near == 2, number(device != position), 2 + number(device != pair))
        slot = jnp.where(lent, slot, 0)
        bias = jnp.where(lent, jnp.float32(0), jnp.float32(MASKED))
        found.append((slot, pl.multiple_of((listed % local_blocks) * BLOCK, BLOCK), bias))
    return found


def weigh_block(query, keys, lanes, found):
    gathered = jnp.concatenate(
        [keys[slot, pl.ds(row, BLOCK), lanes] for slot, row, _ in found], axis=0
    )
    scores = lax.dot_general(
        query, gathered, (((1,), (1,)), ((), ())), preferred_element_type=jnp.float32
    )
    bias = jnp.concatenate([jnp.full((1, BLOCK), part, jnp.float32) for _, _, part in found], axis=1)
    scores = scores + bias
    top = jnp.max(scores, axis=1, keepdims=True)
    weight = jnp.exp2((scores - top) * SCALE)
    total = jnp.sum(weight, axis=1, keepdims=True)
    return top, total, weight.astype(jnp.bfloat16)


def sum_block(weight, values, lanes, found):
    gathered = jnp.concatenate(
        [values[slot, pl.ds(row, BLOCK), lanes] for slot, row, _ in found], axis=0
    )
    return jnp.dot(weight, gathered, preferred_element_type=jnp.float32)


def copied(sources, target, sems, run, begin=0, slots=None):
    first, count = run
    copies = []
    for index, pieces in enumerate(sources):
        slot, start = index if slots is None else slots[index], (first - begin) * DH
        for piece in pieces:
            if 0 <= start < piece.shape[1]:
                copies.append(
                    pltpu.make_async_copy(
                        piece.at[:, pl.ds(start, count * DH)],
                        target.at[slot, :, pl.ds(first * DH, count * DH)],
                        sems.at[index],
                    )
                )
                copies[-1].start()
            start = start - piece.shape[1]
    return copies


def score_kernel(
    entries, local_blocks, keep, groups, pieces, place, kept, queries, *refs
):
    key_tiles, taken = [], 0
    for piece_count in pieces:
        key_tiles.append(refs[taken : taken + piece_count])
        taken += piece_count
    near = [(tile,) for tile in refs[taken:-6]]
    weights, stats, values, keys, key_sems, value_sems = refs[-6:]
    copies = []
    for group, (first, count) in enumerate(groups):
        copies.append(copied(key_tiles, keys, key_sems.at[group], (first, count)))
    value_copies = copied(near, values, value_sems, (0, queries.shape[1] // DH))
    found = [entries(place, kept, block, local_blocks, keep) for block in range(local_blocks)]
    for (first, count), arriving in zip(groups, copies):
        for copy in arriving:
            copy.wait()
        for head in range(first, first + count):
            lanes = pl.ds(head * DH, DH)
            for block in range(local_blocks):
                rows = pl.ds(block * BLOCK, BLOCK)
                top, total, weight = weigh_block(queries[rows, lanes], keys, lanes, found[block])
                weights[head, rows, :] = weight
                stats[0, rows, pl.ds(head, 1)] = top
                stats[1, rows, pl.ds(head, 1)] = total
    for copy in value_copies:
        copy.wait()


def lent_kernel(local_blocks, keep, groups, taken, place, kept, weights, stats, *refs):
    tiles, answers, (values, sems) = refs[:taken], refs[taken:-2], refs[-2:]
    tiles = [(tile,) for tile in tiles[: LENT_TILES - 1]] + [tiles[LENT_TILES - 1 :]]
    copies = []
    for group, run in enumerate(groups):
        copies.append(copied(tiles, values, sems.at[group], run))
    found = [lent_entries(place, kept, block, local_blocks, keep) for block in range(local_blocks)]
    shares = []
    for block in range(local_blocks):
        shares.append(1.0 / stats[1, pl.ds(block * BLOCK, BLOCK), :])
    for (first, count), arriving, answer in zip(groups, copies, answers):
        for copy in arriving:
            copy.wait()
        for head in range(first, first + count):
            lanes = pl.ds(head * DH, DH)
            for block in range(local_blocks):
                rows = pl.ds(block * BLOCK, BLOCK)
                numerator = sum_block(weights[head, rows, :], values, lanes, found[block])
                share = shares[block][:, head : head + 1]
                answer[rows, pl.ds((head - first) * DH, DH)] = (numerator * share).astype(
                    jnp.bfloat16
                )


def value_kernel(
    local_blocks, keep, begin, groups, parts, runs, place, kept, weights, own, lent, *refs
):
    borrowed = dict(zip(runs, refs[1 : 1 + len(runs)]))
    far = refs[1 + len(runs) : 1 + len(runs) + len(FAR) * parts]
    attended, values, result, far_sems, out_sems = refs[-5:]
    far = [far[index * parts : (index + 1) * parts] for index in range(len(FAR))]
    copies = []
    for group, run in enumerate(groups):
        copies.append(copied(far, values, far_sems.at[group], run, begin, FAR))
    found = [own_entries(place, kept, block, local_blocks, keep) for block in range(local_blocks)]
    shares = []
    for block in range(local_blocks):
        rows = pl.ds(block * BLOCK, BLOCK)
        top = jnp.maximum(own[0, rows, :], lent[0, rows, :])
        own_scale = jnp.exp2((own[0, rows, :] - top) * SCALE)
        lent_total = lent[1, rows, :] * jnp.exp2((lent[0, rows, :] - top) * SCALE)
        total = own[1, rows, :] * own_scale + lent_total
        shares.append((own_scale / total, lent_total / total))
    leaving = []
    for group, (first, count) in enumerate(groups):
        for copy in copies[group]:
            copy.wait()
        for head in range(first, first + count):
            lanes = pl.ds(head * DH, DH)
            for block in range(local_blocks):
                rows = pl.ds(block * BLOCK, BLOCK)
                own_share, lent_share = (share[:, head : head + 1] for share in shares[block])
                numerator = sum_block(weights[head, rows, :], values, lanes, found[block])
                run = max(run for run in runs if run <= head)
                answer = borrowed[run][rows, pl.ds((head - run) * DH, DH)]
                whole = numerator * own_share + answer.astype(jnp.float32) * lent_share
                result[rows, pl.ds((head - begin) * DH, DH)] = whole.astype(jnp.bfloat16)
        leaving.append(
            pltpu.make_async_copy(
                result.at[:, pl.ds((first - begin) * DH, count * DH)],
                attended.at[:, pl.ds(first * DH, count * DH)],
                out_sems.at[group],
            )
        )
        leaving[-1].start()
    for copy in leaving:
        copy.wait()


def in_vmem(arrays):
    return [pltpu.with_memory_space_constraint(array, pltpu.VMEM) for array in arrays]


SCALARS = pl.BlockSpec(memory_space=pltpu.SMEM)
HELD = pl.BlockSpec(memory_space=pltpu.VMEM)
ANYWHERE = pl.BlockSpec(memory_space=pl.ANY)


def cost(kept, heads, products, exponentials):
    pairs = kept.shape[0] * kept.shape[1] * heads * BLOCK * BLOCK
    return pl.CostEstimate(
        flops=2 * products * pairs * DH,
        bytes_accessed=2 * products * pairs,
        transcendentals=exponentials * pairs,
    )


def weigh(entries, place, kept, queries, tiles, near, stacked, groups, name):
    rows, columns = queries.shape
    heads = columns // DH
    pieces = [piece for tile in tiles for piece in tile]
    return pl.pallas_call(
        functools.partial(score_kernel, entries, *kept.shape, groups, [len(t) for t in tiles]),
        out_shape=(
            pltpu.VMEM((heads, rows, kept.shape[1] * BLOCK), jnp.bfloat16),
            pltpu.VMEM((2, rows, LANES), jnp.float32),
            pltpu.VMEM((stacked, rows, columns), jnp.bfloat16),
        ),
        in_specs=[SCALARS, SCALARS, HELD] + [ANYWHERE] * (len(pieces) + len(near)),
        out_specs=(HELD, HELD, HELD),
        scratch_shapes=[
            pltpu.VMEM((len(tiles), rows, columns), jnp.bfloat16),
            pltpu.SemaphoreType.DMA((len(groups), len(tiles))),
            pltpu.SemaphoreType.DMA((max(1, len(near)),)),
        ],
        compiler_params=pltpu.CompilerParams(vmem_limit_bytes=14 * 1024 * 1024),
        cost_estimate=cost(kept, heads, 1, 1),
        name=name,
    )(place, kept, *in_vmem((queries,)), *pieces, *near)


def sum_lent(place, kept, weights, stats, tiles, groups):
    heads, rows, _ = weights.shape
    return pl.pallas_call(
        functools.partial(lent_kernel, *kept.shape, groups, len(tiles)),
        out_shape=[
            jax.ShapeDtypeStruct((rows, count * DH), jnp.bfloat16) for _, count in groups
        ],
        in_specs=[SCALARS, SCALARS, HELD, HELD] + [ANYWHERE] * len(tiles),
        out_specs=[HELD] * len(groups),
        scratch_shapes=[
            pltpu.VMEM((LENT_TILES, rows, heads * DH), jnp.bfloat16),
            pltpu.SemaphoreType.DMA((len(groups), LENT_TILES)),
        ],
        compiler_params=pltpu.CompilerParams(vmem_limit_bytes=10 * 1024 * 1024),
        cost_estimate=cost(kept, heads, 1, 0),
        name="sum_lent",
    )(place, kept, *in_vmem((weights, stats)), *tiles)


def combine(place, kept, weights, own, lent, values, borrowed, far, begin, groups, before):
    heads, rows, _ = weights.shape
    pieces = [piece for tile in far for piece in tile]
    last = begin + sum(count for _, count in groups)
    borrowed = [(run, piece) for run, piece in borrowed if begin < run + piece.shape[1] // DH and run < last]
    runs = [run for run, _ in borrowed]
    held = in_vmem((weights, own, lent, values, *(piece for _, piece in borrowed)))
    operands = [place, kept, *held, *pieces]
    in_specs = [SCALARS, SCALARS] + [HELD] * len(held) + [ANYWHERE] * len(pieces)
    aliases = {5: 1}
    if before is not None:
        aliases[len(operands)] = 0
        operands.append(before)
        in_specs.append(ANYWHERE)
    count = sum(count for _, count in groups)
    return pl.pallas_call(
        functools.partial(value_kernel, *kept.shape, begin, groups, len(far[0]), runs),
        out_shape=(
            jax.ShapeDtypeStruct((rows, heads * DH), jnp.bfloat16),
            pltpu.VMEM(values.shape, values.dtype),
        ),
        in_specs=in_specs,
        out_specs=(ANYWHERE, HELD),
        input_output_aliases=aliases,
        scratch_shapes=[
            pltpu.VMEM((rows, count * DH), jnp.bfloat16),
            pltpu.SemaphoreType.DMA((len(groups), len(FAR))),
            pltpu.SemaphoreType.DMA((len(groups),)),
        ],
        compiler_params=pltpu.CompilerParams(vmem_limit_bytes=6 * 1024 * 1024),
        cost_estimate=cost(kept, count, 1, 0),
        name=f"combine_{begin}",
    )(*operands)


def grouped(begin, count, size):
    return [(first, min(size, begin + count - first)) for first in range(begin, begin + count, size)]


def per_device(queries, keys, values, kept):
    position = lax.axis_index("blk").astype(jnp.int32)
    place = position.reshape(1)
    same_side = (position // 2) % 2 == (position // 4) % 2
    heads = queries.shape[1] // DH
    groups = grouped(0, heads, GROUP)

    k_odd, k_even = swapped_odd(keys), swapped(keys, 4)
    asked_kept = swapped(kept, 2)
    k_pair, v_pair = swapped(keys, 1), swapped(values, 1)
    asked = swapped(after(queries, asked_kept, k_pair, v_pair), 2)
    later = after(values, asked_kept, k_pair, v_pair)
    v_odd, v_even = swapped_odd(later), swapped(later, 4)
    k_odd_far, k_even_far = swapped_odd(k_even), swapped(k_odd, 4)
    k_level = jnp.where(same_side, k_even, k_odd)
    v_level = jnp.where(same_side, v_even, v_odd)
    k_pair_level = swapped(after(k_level, asked), 1)
    half = GROUP * (heads // (2 * GROUP)) * DH
    v_pair_level = (swapped(v_level[:, :half], 1), swapped(v_level[:, half:], 1))
    lent_weights, lent_stats, _ = weigh(
        lent_entries, place, asked_kept, asked, ((keys,), (k_level,), (k_pair,), (k_pair_level,)), (), 1,
        groups, "weigh_lent",
    )
    lent = swapped(lent_stats, 2)
    answer = sum_lent(
        place, asked_kept, lent_weights, lent_stats, (values, v_level, v_pair, *v_pair_level), groups
    )
    borrowed = [
        (first, swapped(after(piece, lent), 2)) for (first, _), piece in zip(groups, answer)
    ]
    weights, own, staged = weigh(
        own_entries, place, kept, after(queries, *answer),
        ((keys,), (k_pair,), (k_even,), (k_odd,), (k_even_far,), (k_odd_far,)),
        (values, v_pair, v_even, v_odd), OWN_TILES, groups, "weigh_own",
    )
    attended, begin, hold = None, 0, lent
    hops = []
    for count in VALUE_SPLIT:
        lanes = slice(begin * DH, (begin + count) * DH)
        hops.append(
            (swapped(after(v_odd[:, lanes], hold), 4), swapped_odd(after(v_even[:, lanes], hold)))
        )
        begin, hold = begin + count, own
    begin = 0
    for count, far in zip(VALUE_SPLIT, hops):
        attended, staged = combine(
            place, kept, weights, own, lent, staged, borrowed, tuple((tile,) for tile in far),
            begin, grouped(begin, count, GROUP), attended,
        )
        begin += count
    return attended


def solution(mesh):
    placed = P(("clip", "blk"), None)
    return jax.shard_map(
        per_device, mesh=mesh, in_specs=(placed,) * 4, out_specs=placed, check_vma=False
    )
```

```python
import functools
import math

import jax
import jax.numpy as jnp
from jax import lax
from jax.experimental import pallas as pl
from jax.experimental.pallas import tpu as pltpu
from jax.sharding import PartitionSpec as P

DH = 128
BLOCK = 128
LANES = 128
TOTALS = LANES // 2
VALUE_SPLIT = (15, 5)
GROUP = 5
OWN_TILES = 6
FAR = (4, 5)
LENT_TILES = 4
SCALE = math.log2(math.e) / math.sqrt(DH)
MASKED = -1e30


def permuted(value, target):
    count = lax.axis_size("blk")
    pairs = [(i, target(i)) for i in range(count)]
    return lax.ppermute(value, "blk", [(i, t) for i, t in pairs if 0 <= t < count])


def swapped(value, bit):
    return permuted(value, lambda i: i ^ bit)


def swapped_odd(value):
    return permuted(value, lambda i: i + 4 if i & 4 else i - 4)


def after(value, *earlier):
    return lax.optimization_barrier((value, *earlier))[0]


def number(flag):
    return flag.astype(jnp.int32)


def own_entries(place, kept, block, local_blocks, keep):
    position = place[0]
    pair = position + 1 - 2 * (position % 2)
    level = (position // 4) % 2
    found = []
    for entry in range(keep):
        listed = kept[block, entry]
        device = listed // local_blocks
        offset = device - position
        near = jnp.abs(offset)
        side = 1 - (number(offset > 0) + level) % 2
        slot = jnp.where(near == 8, 4 + side, jnp.where(near == 4, 2 + side, number(device == pair)))
        lent = (near == 2) | ((near == 1) & (device != pair))
        slot = jnp.where(lent, 0, slot)
        bias = jnp.where(lent, jnp.float32(MASKED), jnp.float32(0))
        found.append((slot, pl.multiple_of((listed % local_blocks) * BLOCK, BLOCK), bias))
    return found


def lent_entries(place, kept, block, local_blocks, keep):
    position = place[0]
    client = position + 2 - 4 * ((position // 2) % 2)
    pair = position + 1 - 2 * (position % 2)
    client_pair = client + 1 - 2 * (client % 2)
    found = []
    for entry in range(keep):
        listed = kept[block, entry]
        device = listed // local_blocks
        near = jnp.abs(device - client)
        lent = (near == 2) | ((near == 1) & (device != client_pair))
        slot = jnp.where(near == 2, number(device != position), 2 + number(device != pair))
        slot = jnp.where(lent, slot, 0)
        bias = jnp.where(lent, jnp.float32(0), jnp.float32(MASKED))
        found.append((slot, pl.multiple_of((listed % local_blocks) * BLOCK, BLOCK), bias))
    return found


def weigh_block(query, keys, lanes, found):
    gathered = jnp.concatenate(
        [keys[slot, pl.ds(row, BLOCK), lanes] for slot, row, _ in found], axis=0
    )
    scores = lax.dot_general(
        query, gathered, (((1,), (1,)), ((), ())), preferred_element_type=jnp.float32
    )
    bias = jnp.concatenate([jnp.full((1, BLOCK), part, jnp.float32) for _, _, part in found], axis=1)
    scores = scores + bias
    top = jnp.max(scores, axis=1, keepdims=True)
    weight = jnp.exp2((scores - top) * SCALE)
    total = jnp.sum(weight, axis=1, keepdims=True)
    return top, total, weight.astype(jnp.bfloat16)


def sum_block(weight, values, lanes, found):
    gathered = jnp.concatenate(
        [values[slot, pl.ds(row, BLOCK), lanes] for slot, row, _ in found], axis=0
    )
    return jnp.dot(weight, gathered, preferred_element_type=jnp.float32)


def copied(sources, target, sems, run, begin=0, slots=None):
    first, count = run
    copies = []
    for index, pieces in enumerate(sources):
        slot, start = index if slots is None else slots[index], (first - begin) * DH
        for piece in pieces:
            if 0 <= start < piece.shape[1]:
                copies.append(
                    pltpu.make_async_copy(
                        piece.at[:, pl.ds(start, count * DH)],
                        target.at[slot, :, pl.ds(first * DH, count * DH)],
                        sems.at[index],
                    )
                )
                copies[-1].start()
            start = start - piece.shape[1]
    return copies


def score_kernel(
    entries, local_blocks, keep, groups, pieces, place, kept, queries, *refs
):
    key_tiles, taken = [], 0
    for piece_count in pieces:
        key_tiles.append(refs[taken : taken + piece_count])
        taken += piece_count
    near = [(tile,) for tile in refs[taken:-6]]
    weights, stats, values, keys, key_sems, value_sems = refs[-6:]
    copies = []
    for group, (first, count) in enumerate(groups):
        copies.append(copied(key_tiles, keys, key_sems.at[group], (first, count)))
    value_copies = copied(near, values, value_sems, (0, queries.shape[1] // DH))
    found = [entries(place, kept, block, local_blocks, keep) for block in range(local_blocks)]
    for (first, count), arriving in zip(groups, copies):
        for copy in arriving:
            copy.wait()
        for head in range(first, first + count):
            lanes = pl.ds(head * DH, DH)
            for block in range(local_blocks):
                rows = pl.ds(block * BLOCK, BLOCK)
                top, total, weight = weigh_block(queries[rows, lanes], keys, lanes, found[block])
                weights[head, rows, :] = weight
                stats[rows, pl.ds(head, 1)] = top
                stats[rows, pl.ds(TOTALS + head, 1)] = total
    for copy in value_copies:
        copy.wait()


def lent_kernel(local_blocks, keep, groups, taken, place, kept, weights, stats, *refs):
    tiles, answers, (values, sems) = refs[:taken], refs[taken:-2], refs[-2:]
    tiles = [(tile,) for tile in tiles[: LENT_TILES - 1]] + [tiles[LENT_TILES - 1 :]]
    copies = []
    for group, run in enumerate(groups):
        copies.append(copied(tiles, values, sems.at[group], run))
    found = [lent_entries(place, kept, block, local_blocks, keep) for block in range(local_blocks)]
    shares = []
    for block in range(local_blocks):
        shares.append(1.0 / stats[pl.ds(block * BLOCK, BLOCK), pl.ds(TOTALS, TOTALS)])
    for (first, count), arriving, answer in zip(groups, copies, answers):
        for copy in arriving:
            copy.wait()
        for head in range(first, first + count):
            lanes = pl.ds(head * DH, DH)
            for block in range(local_blocks):
                rows = pl.ds(block * BLOCK, BLOCK)
                numerator = sum_block(weights[head, rows, :], values, lanes, found[block])
                share = shares[block][:, head : head + 1]
                answer[rows, pl.ds((head - first) * DH, DH)] = (numerator * share).astype(
                    jnp.bfloat16
                )


def value_kernel(
    local_blocks, keep, begin, groups, parts, runs, direct, place, kept, weights, own, lent, *refs
):
    borrowed = dict(zip(runs, refs[1 : 1 + len(runs)]))
    far = refs[1 + len(runs) : 1 + len(runs) + len(FAR) * parts]
    attended, values, result, far_sems, out_sems = refs[-5:]
    far = [far[index * parts : (index + 1) * parts] for index in range(len(FAR))]
    copies = []
    for group, run in enumerate(groups):
        if direct:
            first, count = run
            for slot, (piece,) in zip(FAR, far):
                values[slot, :, pl.ds(first * DH, count * DH)] = piece[
                    :, pl.ds((first - begin) * DH, count * DH)
                ]
            copies.append([])
        else:
            copies.append(copied(far, values, far_sems.at[group], run, begin, FAR))
    found = [own_entries(place, kept, block, local_blocks, keep) for block in range(local_blocks)]
    shares = []
    for block in range(local_blocks):
        rows = pl.ds(block * BLOCK, BLOCK)
        own_top, lent_top = own[rows, pl.ds(0, TOTALS)], lent[rows, pl.ds(0, TOTALS)]
        top = jnp.maximum(own_top, lent_top)
        own_scale = jnp.exp2((own_top - top) * SCALE)
        lent_scale = jnp.exp2((lent_top - top) * SCALE)
        lent_total = lent[rows, pl.ds(TOTALS, TOTALS)] * lent_scale
        total = own[rows, pl.ds(TOTALS, TOTALS)] * own_scale + lent_total
        shares.append((own_scale / total, lent_total / total))
    leaving = []
    for group, (first, count) in enumerate(groups):
        for copy in copies[group]:
            copy.wait()
        for head in range(first, first + count):
            lanes = pl.ds(head * DH, DH)
            for block in range(local_blocks):
                rows = pl.ds(block * BLOCK, BLOCK)
                own_share, lent_share = (share[:, head : head + 1] for share in shares[block])
                numerator = sum_block(weights[head, rows, :], values, lanes, found[block])
                run = max(run for run in runs if run <= head)
                answer = borrowed[run][rows, pl.ds((head - run) * DH, DH)]
                whole = numerator * own_share + answer.astype(jnp.float32) * lent_share
                result[rows, pl.ds((head - begin) * DH, DH)] = whole.astype(jnp.bfloat16)
        leaving.append(
            pltpu.make_async_copy(
                result.at[:, pl.ds((first - begin) * DH, count * DH)],
                attended.at[:, pl.ds(first * DH, count * DH)],
                out_sems.at[group],
            )
        )
        leaving[-1].start()
    for copy in leaving:
        copy.wait()


def in_vmem(arrays):
    return [pltpu.with_memory_space_constraint(array, pltpu.VMEM) for array in arrays]


SCALARS = pl.BlockSpec(memory_space=pltpu.SMEM)
HELD = pl.BlockSpec(memory_space=pltpu.VMEM)
ANYWHERE = pl.BlockSpec(memory_space=pl.ANY)


def cost(kept, heads, products, exponentials):
    pairs = kept.shape[0] * kept.shape[1] * heads * BLOCK * BLOCK
    return pl.CostEstimate(
        flops=2 * products * pairs * DH,
        bytes_accessed=2 * products * pairs,
        transcendentals=exponentials * pairs,
    )


def weigh(entries, place, kept, queries, tiles, near, stacked, groups, name):
    rows, columns = queries.shape
    heads = columns // DH
    pieces = [piece for tile in tiles for piece in tile]
    return pl.pallas_call(
        functools.partial(score_kernel, entries, *kept.shape, groups, [len(t) for t in tiles]),
        out_shape=(
            pltpu.VMEM((heads, rows, kept.shape[1] * BLOCK), jnp.bfloat16),
            pltpu.VMEM((rows, LANES), jnp.float32),
            pltpu.VMEM((stacked, rows, columns), jnp.bfloat16),
        ),
        in_specs=[SCALARS, SCALARS, HELD] + [ANYWHERE] * (len(pieces) + len(near)),
        out_specs=(HELD, HELD, HELD),
        scratch_shapes=[
            pltpu.VMEM((len(tiles), rows, columns), jnp.bfloat16),
            pltpu.SemaphoreType.DMA((len(groups), len(tiles))),
            pltpu.SemaphoreType.DMA((max(1, len(near)),)),
        ],
        compiler_params=pltpu.CompilerParams(vmem_limit_bytes=14 * 1024 * 1024),
        cost_estimate=cost(kept, heads, 1, 1),
        name=name,
    )(place, kept, *in_vmem((queries,)), *pieces, *near)


def sum_lent(place, kept, weights, stats, tiles, groups):
    heads, rows, _ = weights.shape
    return pl.pallas_call(
        functools.partial(lent_kernel, *kept.shape, groups, len(tiles)),
        out_shape=[
            jax.ShapeDtypeStruct((rows, count * DH), jnp.bfloat16) for _, count in groups
        ],
        in_specs=[SCALARS, SCALARS, HELD, HELD] + [ANYWHERE] * len(tiles),
        out_specs=[HELD] * len(groups),
        scratch_shapes=[
            pltpu.VMEM((LENT_TILES, rows, heads * DH), jnp.bfloat16),
            pltpu.SemaphoreType.DMA((len(groups), LENT_TILES)),
        ],
        compiler_params=pltpu.CompilerParams(vmem_limit_bytes=10 * 1024 * 1024),
        cost_estimate=cost(kept, heads, 1, 0),
        name="sum_lent",
    )(place, kept, *in_vmem((weights, stats)), *tiles)


def combine(place, kept, weights, own, lent, values, borrowed, far, begin, groups, before):
    heads, rows, _ = weights.shape
    pieces = [piece for tile in far for piece in tile]
    last = begin + sum(count for _, count in groups)
    borrowed = [(run, piece) for run, piece in borrowed if begin < run + piece.shape[1] // DH and run < last]
    runs = [run for run, _ in borrowed]
    held = in_vmem((weights, own, lent, values, *(piece for _, piece in borrowed)))
    direct = before is not None
    operands = [place, kept, *held, *(in_vmem(pieces) if direct else pieces)]
    in_specs = [SCALARS, SCALARS] + [HELD] * len(held)
    in_specs += [HELD if direct else ANYWHERE] * len(pieces)
    aliases = {5: 1}
    if before is not None:
        aliases[len(operands)] = 0
        operands.append(before)
        in_specs.append(ANYWHERE)
    count = sum(count for _, count in groups)
    return pl.pallas_call(
        functools.partial(value_kernel, *kept.shape, begin, groups, len(far[0]), runs, direct),
        out_shape=(
            jax.ShapeDtypeStruct((rows, heads * DH), jnp.bfloat16),
            pltpu.VMEM(values.shape, values.dtype),
        ),
        in_specs=in_specs,
        out_specs=(ANYWHERE, HELD),
        input_output_aliases=aliases,
        scratch_shapes=[
            pltpu.VMEM((rows, count * DH), jnp.bfloat16),
            pltpu.SemaphoreType.DMA((len(groups), len(FAR))),
            pltpu.SemaphoreType.DMA((len(groups),)),
        ],
        compiler_params=pltpu.CompilerParams(vmem_limit_bytes=6 * 1024 * 1024),
        cost_estimate=cost(kept, count, 1, 0),
        name=f"combine_{begin}",
    )(*operands)


def grouped(begin, count, size):
    return [(first, min(size, begin + count - first)) for first in range(begin, begin + count, size)]


def per_device(queries, keys, values, kept):
    position = lax.axis_index("blk").astype(jnp.int32)
    place = position.reshape(1)
    same_side = (position // 2) % 2 == (position // 4) % 2
    heads = queries.shape[1] // DH
    groups = grouped(0, heads, GROUP)

    k_odd, k_even = swapped_odd(keys), swapped(keys, 4)
    asked_kept = swapped(kept, 2)
    k_pair, v_pair = swapped(keys, 1), swapped(values, 1)
    asked = swapped(after(queries, asked_kept, k_pair, v_pair), 2)
    later = after(values, asked_kept, k_pair, v_pair)
    v_odd, v_even = swapped_odd(later), swapped(later, 4)
    k_odd_far, k_even_far = swapped_odd(k_even), swapped(k_odd, 4)
    k_level = jnp.where(same_side, k_even, k_odd)
    v_level = jnp.where(same_side, v_even, v_odd)
    k_pair_level = swapped(after(k_level, asked), 1)
    half = GROUP * (heads // (2 * GROUP)) * DH
    v_pair_level = (swapped(v_level[:, :half], 1), swapped(v_level[:, half:], 1))
    lent_weights, lent_stats, _ = weigh(
        lent_entries, place, asked_kept, asked, ((keys,), (k_level,), (k_pair,), (k_pair_level,)), (), 1,
        groups, "weigh_lent",
    )
    lent = swapped(lent_stats, 2)
    answer = sum_lent(
        place, asked_kept, lent_weights, lent_stats, (values, v_level, v_pair, *v_pair_level), groups
    )
    borrowed = [
        (first, swapped(after(piece, lent), 2)) for (first, _), piece in zip(groups, answer)
    ]
    weights, own, staged = weigh(
        own_entries, place, kept, after(queries, *answer),
        ((keys,), (k_pair,), (k_even,), (k_odd,), (k_even_far,), (k_odd_far,)),
        (values, v_pair, v_even, v_odd), OWN_TILES, groups, "weigh_own",
    )
    attended, begin, hold = None, 0, lent
    hops = []
    for count in VALUE_SPLIT:
        lanes = slice(begin * DH, (begin + count) * DH)
        hops.append(
            (swapped(after(v_odd[:, lanes], hold), 4), swapped_odd(after(v_even[:, lanes], hold)))
        )
        begin, hold = begin + count, own
    begin = 0
    for count, far in zip(VALUE_SPLIT, hops):
        attended, staged = combine(
            place, kept, weights, own, lent, staged, borrowed, tuple((tile,) for tile in far),
            begin, grouped(begin, count, GROUP), attended,
        )
        begin += count
    return attended


def solution(mesh):
    placed = P(("clip", "blk"), None)
    return jax.shard_map(
        per_device, mesh=mesh, in_specs=(placed,) * 4, out_specs=placed, check_vma=False
    )
```

```python
import functools
import math

import jax
import jax.numpy as jnp
from jax import lax
from jax.experimental import pallas as pl
from jax.experimental.pallas import tpu as pltpu
from jax.sharding import PartitionSpec as P

DH = 128
BLOCK = 128
LANES = 128
TOTALS = LANES // 2
VALUE_SPLIT = (15, 5)
GROUP = 5
OWN_TILES = 6
FAR = (4, 5)
LENT_TILES = 4
SCALE = math.log2(math.e) / math.sqrt(DH)
MASKED = -1e30


def permuted(value, target):
    count = lax.axis_size("blk")
    pairs = [(i, target(i)) for i in range(count)]
    return lax.ppermute(value, "blk", [(i, t) for i, t in pairs if 0 <= t < count])


def swapped(value, bit):
    return permuted(value, lambda i: i ^ bit)


def swapped_odd(value):
    return permuted(value, lambda i: i + 4 if i & 4 else i - 4)


def after(value, *earlier):
    return lax.optimization_barrier((value, *earlier))[0]


def number(flag):
    return flag.astype(jnp.int32)


def own_entries(place, kept, block, local_blocks, keep):
    position = place[0]
    pair = position + 1 - 2 * (position % 2)
    level = (position // 4) % 2
    found = []
    for entry in range(keep):
        listed = kept[block, entry]
        device = listed // local_blocks
        offset = device - position
        near = jnp.abs(offset)
        side = 1 - (number(offset > 0) + level) % 2
        slot = jnp.where(near == 8, 4 + side, jnp.where(near == 4, 2 + side, number(device == pair)))
        lent = (near == 2) | ((near == 1) & (device != pair))
        slot = jnp.where(lent, 0, slot)
        bias = jnp.where(lent, jnp.float32(MASKED), jnp.float32(0))
        found.append((slot, pl.multiple_of((listed % local_blocks) * BLOCK, BLOCK), bias))
    return found


def lent_entries(place, kept, block, local_blocks, keep):
    position = place[0]
    client = position + 2 - 4 * ((position // 2) % 2)
    pair = position + 1 - 2 * (position % 2)
    client_pair = client + 1 - 2 * (client % 2)
    found = []
    for entry in range(keep):
        listed = kept[block, entry]
        device = listed // local_blocks
        near = jnp.abs(device - client)
        lent = (near == 2) | ((near == 1) & (device != client_pair))
        slot = jnp.where(near == 2, number(device != position), 2 + number(device != pair))
        slot = jnp.where(lent, slot, 0)
        bias = jnp.where(lent, jnp.float32(0), jnp.float32(MASKED))
        found.append((slot, pl.multiple_of((listed % local_blocks) * BLOCK, BLOCK), bias))
    return found


def weigh_block(query, keys, lanes, found):
    gathered = jnp.concatenate(
        [keys[slot, pl.ds(row, BLOCK), lanes] for slot, row, _ in found], axis=0
    )
    scores = lax.dot_general(
        query, gathered, (((1,), (1,)), ((), ())), preferred_element_type=jnp.float32
    )
    bias = jnp.concatenate([jnp.full((1, BLOCK), part, jnp.float32) for _, _, part in found], axis=1)
    scores = scores + bias
    top = jnp.max(scores, axis=1, keepdims=True)
    weight = jnp.exp2((scores - top) * SCALE)
    total = jnp.sum(weight, axis=1, keepdims=True)
    return top, total, weight.astype(jnp.bfloat16)


def sum_block(weight, values, lanes, found):
    gathered = jnp.concatenate(
        [values[slot, pl.ds(row, BLOCK), lanes] for slot, row, _ in found], axis=0
    )
    return jnp.dot(weight, gathered, preferred_element_type=jnp.float32)


def copied(sources, target, sems, run, begin=0, slots=None):
    first, count = run
    copies = []
    for index, pieces in enumerate(sources):
        slot, start = index if slots is None else slots[index], (first - begin) * DH
        for piece in pieces:
            if 0 <= start < piece.shape[1]:
                copies.append(
                    pltpu.make_async_copy(
                        piece.at[:, pl.ds(start, count * DH)],
                        target.at[slot, :, pl.ds(first * DH, count * DH)],
                        sems.at[index],
                    )
                )
                copies[-1].start()
            start = start - piece.shape[1]
    return copies


def score_kernel(
    entries, local_blocks, keep, groups, pieces, place, kept, queries, *refs
):
    key_tiles, taken = [], 0
    for piece_count in pieces:
        key_tiles.append(refs[taken : taken + piece_count])
        taken += piece_count
    near = [(tile,) for tile in refs[taken:-6]]
    weights, stats, values, keys, key_sems, value_sems = refs[-6:]
    copies = []
    for group, (first, count) in enumerate(groups):
        copies.append(copied(key_tiles, keys, key_sems.at[group], (first, count)))
    value_copies = copied(near, values, value_sems, (0, queries.shape[1] // DH))
    found = [entries(place, kept, block, local_blocks, keep) for block in range(local_blocks)]
    for (first, count), arriving in zip(groups, copies):
        for copy in arriving:
            copy.wait()
        for head in range(first, first + count):
            lanes = pl.ds(head * DH, DH)
            for block in range(local_blocks):
                rows = pl.ds(block * BLOCK, BLOCK)
                top, total, weight = weigh_block(queries[rows, lanes], keys, lanes, found[block])
                weights[head, rows, :] = weight
                stats[rows, pl.ds(head, 1)] = top
                stats[rows, pl.ds(TOTALS + head, 1)] = total
    for copy in value_copies:
        copy.wait()


def lent_kernel(local_blocks, keep, groups, taken, place, kept, weights, stats, *refs):
    tiles, answers, (values, sems) = refs[:taken], refs[taken:-2], refs[-2:]
    tiles = [(tile,) for tile in tiles[: LENT_TILES - 1]] + [tiles[LENT_TILES - 1 :]]
    copies = []
    for group, run in enumerate(groups):
        copies.append(copied(tiles, values, sems.at[group], run))
    found = [lent_entries(place, kept, block, local_blocks, keep) for block in range(local_blocks)]
    shares = []
    for block in range(local_blocks):
        shares.append(1.0 / stats[pl.ds(block * BLOCK, BLOCK), pl.ds(TOTALS, TOTALS)])
    for (first, count), arriving, answer in zip(groups, copies, answers):
        for copy in arriving:
            copy.wait()
        for head in range(first, first + count):
            lanes = pl.ds(head * DH, DH)
            for block in range(local_blocks):
                rows = pl.ds(block * BLOCK, BLOCK)
                numerator = sum_block(weights[head, rows, :], values, lanes, found[block])
                share = shares[block][:, head : head + 1]
                answer[rows, pl.ds((head - first) * DH, DH)] = (numerator * share).astype(
                    jnp.bfloat16
                )


def value_kernel(
    local_blocks, keep, begin, groups, parts, runs, direct, place, kept, weights, own, lent, *refs
):
    borrowed = dict(zip(runs, refs[1 : 1 + len(runs)]))
    far = refs[1 + len(runs) : 1 + len(runs) + len(FAR) * parts]
    attended, values, result, far_sems, out_sems = refs[-5:]
    far = [far[index * parts : (index + 1) * parts] for index in range(len(FAR))]
    copies = []
    for group, run in enumerate(groups):
        if direct:
            first, count = run
            for slot, (piece,) in zip(FAR, far):
                values[slot, :, pl.ds(first * DH, count * DH)] = piece[
                    :, pl.ds((first - begin) * DH, count * DH)
                ]
            copies.append([])
        else:
            copies.append(copied(far, values, far_sems.at[group], run, begin, FAR))
    found = [own_entries(place, kept, block, local_blocks, keep) for block in range(local_blocks)]
    shares = []
    for block in range(local_blocks):
        rows = pl.ds(block * BLOCK, BLOCK)
        own_top, lent_top = own[rows, pl.ds(0, TOTALS)], lent[rows, pl.ds(0, TOTALS)]
        top = jnp.maximum(own_top, lent_top)
        own_scale = jnp.exp2((own_top - top) * SCALE)
        lent_scale = jnp.exp2((lent_top - top) * SCALE)
        lent_total = lent[rows, pl.ds(TOTALS, TOTALS)] * lent_scale
        total = own[rows, pl.ds(TOTALS, TOTALS)] * own_scale + lent_total
        shares.append((own_scale / total, lent_total / total))
    leaving = []
    for group, (first, count) in enumerate(groups):
        for copy in copies[group]:
            copy.wait()
        for head in range(first, first + count):
            lanes = pl.ds(head * DH, DH)
            for block in range(local_blocks):
                rows = pl.ds(block * BLOCK, BLOCK)
                own_share, lent_share = (share[:, head : head + 1] for share in shares[block])
                numerator = sum_block(weights[head, rows, :], values, lanes, found[block])
                run = max(run for run in runs if run <= head)
                answer = borrowed[run][rows, pl.ds((head - run) * DH, DH)]
                whole = numerator * own_share + answer.astype(jnp.float32) * lent_share
                result[rows, pl.ds((head - begin) * DH, DH)] = whole.astype(jnp.bfloat16)
        leaving.append(
            pltpu.make_async_copy(
                result.at[:, pl.ds((first - begin) * DH, count * DH)],
                attended.at[:, pl.ds(first * DH, count * DH)],
                out_sems.at[group],
            )
        )
        leaving[-1].start()
    for copy in leaving:
        copy.wait()


def in_vmem(arrays):
    return [pltpu.with_memory_space_constraint(array, pltpu.VMEM) for array in arrays]


SCALARS = pl.BlockSpec(memory_space=pltpu.SMEM)
HELD = pl.BlockSpec(memory_space=pltpu.VMEM)
ANYWHERE = pl.BlockSpec(memory_space=pl.ANY)


def cost(kept, heads, products, exponentials):
    pairs = kept.shape[0] * kept.shape[1] * heads * BLOCK * BLOCK
    return pl.CostEstimate(
        flops=2 * products * pairs * DH,
        bytes_accessed=2 * products * pairs,
        transcendentals=exponentials * pairs,
    )


def weigh(entries, place, kept, queries, tiles, near, stacked, groups, name):
    rows, columns = queries.shape
    heads = columns // DH
    pieces = [piece for tile in tiles for piece in tile]
    return pl.pallas_call(
        functools.partial(score_kernel, entries, *kept.shape, groups, [len(t) for t in tiles]),
        out_shape=(
            pltpu.VMEM((heads, rows, kept.shape[1] * BLOCK), jnp.bfloat16),
            pltpu.VMEM((rows, LANES), jnp.float32),
            pltpu.VMEM((stacked, rows, columns), jnp.bfloat16),
        ),
        in_specs=[SCALARS, SCALARS, HELD] + [ANYWHERE] * (len(pieces) + len(near)),
        out_specs=(HELD, HELD, HELD),
        scratch_shapes=[
            pltpu.VMEM((len(tiles), rows, columns), jnp.bfloat16),
            pltpu.SemaphoreType.DMA((len(groups), len(tiles))),
            pltpu.SemaphoreType.DMA((max(1, len(near)),)),
        ],
        compiler_params=pltpu.CompilerParams(vmem_limit_bytes=14 * 1024 * 1024),
        cost_estimate=cost(kept, heads, 1, 1),
        name=name,
    )(place, kept, *in_vmem((queries,)), *pieces, *near)


def sum_lent(place, kept, weights, stats, tiles, groups):
    heads, rows, _ = weights.shape
    return pl.pallas_call(
        functools.partial(lent_kernel, *kept.shape, groups, len(tiles)),
        out_shape=[
            jax.ShapeDtypeStruct((rows, count * DH), jnp.bfloat16) for _, count in groups
        ],
        in_specs=[SCALARS, SCALARS, HELD, HELD] + [ANYWHERE] * len(tiles),
        out_specs=[HELD] * len(groups),
        scratch_shapes=[
            pltpu.VMEM((LENT_TILES, rows, heads * DH), jnp.bfloat16),
            pltpu.SemaphoreType.DMA((len(groups), LENT_TILES)),
        ],
        compiler_params=pltpu.CompilerParams(vmem_limit_bytes=10 * 1024 * 1024),
        cost_estimate=cost(kept, heads, 1, 0),
        name="sum_lent",
    )(place, kept, *in_vmem((weights, stats)), *tiles)


def combine(place, kept, weights, own, lent, values, borrowed, far, begin, groups, before):
    heads, rows, _ = weights.shape
    pieces = [piece for tile in far for piece in tile]
    last = begin + sum(count for _, count in groups)
    borrowed = [(run, piece) for run, piece in borrowed if begin < run + piece.shape[1] // DH and run < last]
    runs = [run for run, _ in borrowed]
    held = in_vmem((weights, own, lent, values, *(piece for _, piece in borrowed)))
    direct = before is not None
    operands = [place, kept, *held, *(in_vmem(pieces) if direct else pieces)]
    in_specs = [SCALARS, SCALARS] + [HELD] * len(held)
    in_specs += [HELD if direct else ANYWHERE] * len(pieces)
    aliases = {5: 1}
    if before is not None:
        aliases[len(operands)] = 0
        operands.append(before)
        in_specs.append(ANYWHERE)
    count = sum(count for _, count in groups)
    return pl.pallas_call(
        functools.partial(value_kernel, *kept.shape, begin, groups, len(far[0]), runs, direct),
        out_shape=(
            jax.ShapeDtypeStruct((rows, heads * DH), jnp.bfloat16),
            pltpu.VMEM(values.shape, values.dtype),
        ),
        in_specs=in_specs,
        out_specs=(ANYWHERE, HELD),
        input_output_aliases=aliases,
        scratch_shapes=[
            pltpu.VMEM((rows, count * DH), jnp.bfloat16),
            pltpu.SemaphoreType.DMA((len(groups), len(FAR))),
            pltpu.SemaphoreType.DMA((len(groups),)),
        ],
        compiler_params=pltpu.CompilerParams(vmem_limit_bytes=6 * 1024 * 1024),
        cost_estimate=cost(kept, count, 1, 0),
        name=f"combine_{begin}",
    )(*operands)


def grouped(begin, count, size):
    return [(first, min(size, begin + count - first)) for first in range(begin, begin + count, size)]


def per_device(queries, keys, values, kept):
    position = lax.axis_index("blk").astype(jnp.int32)
    place = position.reshape(1)
    same_side = (position // 2) % 2 == (position // 4) % 2
    heads = queries.shape[1] // DH
    groups = grouped(0, heads, GROUP)

    k_odd, k_even = swapped_odd(keys), swapped(keys, 4)
    asked_kept = swapped(kept, 2)
    v_pair = swapped(values, 1)
    k_pair = swapped(after(keys, k_even, k_odd), 1)
    asked = swapped(after(queries, asked_kept, v_pair), 2)
    later = after(values, asked_kept, v_pair)
    v_odd, v_even = swapped_odd(later), swapped(later, 4)
    k_odd_far, k_even_far = swapped_odd(k_even), swapped(k_odd, 4)
    k_level = jnp.where(same_side, k_even, k_odd)
    v_level = jnp.where(same_side, v_even, v_odd)
    k_pair_level = swapped(after(k_level, asked), 1)
    half = GROUP * (heads // (2 * GROUP)) * DH
    v_pair_level = (swapped(v_level[:, :half], 1), swapped(v_level[:, half:], 1))
    lent_weights, lent_stats, _ = weigh(
        lent_entries, place, asked_kept, asked, ((keys,), (k_level,), (k_pair,), (k_pair_level,)), (), 1,
        groups, "weigh_lent",
    )
    lent = swapped(lent_stats, 2)
    answer = sum_lent(
        place, asked_kept, lent_weights, lent_stats, (values, v_level, v_pair, *v_pair_level), groups
    )
    borrowed = [
        (first, swapped(after(piece, lent), 2)) for (first, _), piece in zip(groups, answer)
    ]
    weights, own, staged = weigh(
        own_entries, place, kept, after(queries, *answer),
        ((keys,), (k_pair,), (k_even,), (k_odd,), (k_even_far,), (k_odd_far,)),
        (values, v_pair, v_even, v_odd), OWN_TILES, groups, "weigh_own",
    )
    attended, begin, hold = None, 0, lent
    hops = []
    for count in VALUE_SPLIT:
        lanes = slice(begin * DH, (begin + count) * DH)
        hops.append(
            (swapped(after(v_odd[:, lanes], hold), 4), swapped_odd(after(v_even[:, lanes], hold)))
        )
        begin, hold = begin + count, own
    begin = 0
    for count, far in zip(VALUE_SPLIT, hops):
        attended, staged = combine(
            place, kept, weights, own, lent, staged, borrowed, tuple((tile,) for tile in far),
            begin, grouped(begin, count, GROUP), attended,
        )
        begin += count
    return attended


def solution(mesh):
    placed = P(("clip", "blk"), None)
    return jax.shard_map(
        per_device, mesh=mesh, in_specs=(placed,) * 4, out_specs=placed, check_vma=False
    )
```
